128 devices in a mesh: dom: 8 (over z, core), shard: 16 (over y, x).
Axes of the slice: x: 4, y: 4, z: 4, core: 2. Of those that a mesh axis runs over, the one named last changes fastest.
Arguments:
- features: bfloat16 [65536, 512], P(('dom', 'shard')), may hold values from -6 to 6
- tile_values: bfloat16 [128, 48, 128, 128], P(('dom', 'shard')), may hold values from -0.5 to 0.5
- tile_coords: int32 [128, 48, 2], P(('dom', 'shard')), may hold values from 0 to 7, as said below
- tile_count: int32 [128], P(('dom', 'shard')), may hold values from 8 to 48, as said below
- boundary_index: int32 [128, 8], P(('dom', 'shard')), may hold values from 0 to 511
- peer_pick: int32 [128, 128, 4], P(('dom', 'shard')), may hold values from 0 to 7
- shuffle_order: int32 [128, 512], P(('dom', 'shard')), may hold values from 0 to 511, each once within a row
- attn_weight: bfloat16 [1, 4, 512, 512], replicated, may hold values from -0.25 to 0.25
- ffn_in: bfloat16 [1, 512, 1024], replicated, may hold values from -0.25 to 0.25
- ffn_out: bfloat16 [1, 1024, 512], replicated, may hold values from -0.1875 to 0.1875
- norm_gain: float32 [1, 2, 512], replicated, may hold values from 0.1 to 1.9
- read_weight: float32 [2, 512], replicated, may hold values from -0.1875 to 0.1875
Outputs:
- node_states: bfloat16 [65536, 512], P(('dom', 'shard'))
The draws below stay inside these ranges and needn't reach their ends.
Inputs may be any that keep to these rules, and one draw needn't show every extreme that they name: `tile_coords`: slot r < 4 of every device holds (r, r); slot 4 + j for j < 4 has column block 4 + j; column blocks below 4 are the device's own rows, the others its rows taken from other devices. Slots from tile_count[p] on are unused; some device uses all 48 slots.
All inputs are finite; a program needn't handle non-finite values.
Results may differ from the reference program's by a relative error of at most 0.012.
Values may be sent and summed in bfloat16 or wider, within the bound.
A program may use at most 192 MiB of HBM per device.

```python
import jax
import jax.numpy as jnp
from jax import lax

WIDTH = 512
FFN_HIDDEN = 1024
HEADS = 8
HOPS = 4
LAYERS = 1
TILE = 128
ROWS_DEV = 512
BOUNDARY = 8
PEER_ROWS = 4
TILES_DEV = 48
NODES = 65536
ROW_TILES = 4
HALO_ROWS = 512
HALO_BLOCKS = 4
SHARE = 32
N_DOM = 8
N_SHARD = 16
DEVICES = 128


def draw_tile_coords(key, part):
    key = jax.random.fold_in(key, 11)
    first_key, second_key = jax.random.split(key, 2)
    base_slots = ROW_TILES + HALO_BLOCKS
    rows_any = jax.random.randint(first_key, (DEVICES, TILES_DEV), 0, ROW_TILES)
    cols_any = jax.random.randint(second_key, (DEVICES, TILES_DEV), 0, base_slots)
    slot_index = jnp.broadcast_to(jnp.arange(TILES_DEV)[None, :], (DEVICES, TILES_DEV))
    diagonal = slot_index < ROW_TILES
    covering = (slot_index >= ROW_TILES) & (slot_index < base_slots)
    row_part = jnp.where(diagonal, slot_index, rows_any)
    col_part = jnp.where(diagonal | covering, slot_index, cols_any)
    return jnp.stack([row_part, col_part], -1).astype(jnp.int32)


def draw_tile_count(key, part):
    key = jax.random.fold_in(key, 23)
    first_key, second_key = jax.random.split(key, 2)
    base_slots = ROW_TILES + HALO_BLOCKS
    span_slots = TILES_DEV - base_slots
    raw_draw = jax.random.randint(first_key, (DEVICES,), 0, span_slots + 1)
    extra_slots = raw_draw * raw_draw * raw_draw // (span_slots * span_slots)
    busiest = jax.random.randint(second_key, (), 0, DEVICES)
    counted = jnp.where(jnp.arange(DEVICES) == busiest, TILES_DEV, base_slots + extra_slots)
    return counted.astype(jnp.int32)


def place_ends(entries, key, smallest, high):
    spot = [jax.random.randint(jax.random.fold_in(key, axis), (), 0, length) for axis, length in enumerate(entries.shape)]
    main_axis = entries.shape.index(max(entries.shape))
    next_to = spot[:main_axis] + [(spot[main_axis] + 1) % entries.shape[main_axis]] + spot[main_axis + 1:]
    return entries.at[tuple(spot)].set(smallest).at[tuple(next_to)].set(high)


def shard_levels(rng, extent, shards, least, high):
    level = 1.0
    for position, blocks in shards:
        draws = jax.random.uniform(jax.random.fold_in(jax.random.fold_in(rng, 6), position), (blocks,), jnp.float32, least / len(shards), high / len(shards))
        level = level * jnp.repeat(jnp.exp(draws), extent[position] // blocks).reshape((-1,) + (1,) * (len(extent) - 1 - position))
    return level


def scatter_about(stream_key, shape, scale, bound, cuts=(), dtype=jnp.bfloat16):
    entries = scale * jax.random.normal(stream_key, shape, jnp.float32)
    if cuts:
        entries = entries * shard_levels(stream_key, shape, cuts, -0.22, 0.18)
    return jnp.clip(entries, -bound, bound).astype(dtype)


def setup_inputs(seed: int = 0) -> dict:
    arg_keys = jax.random.split(jax.random.key(seed), 13)
    return {
        "features": scatter_about(arg_keys[0], (NODES, WIDTH), 1.0, 6.0, ((0, 128),)),
        "tile_values": scatter_about(arg_keys[1], (DEVICES, TILES_DEV, TILE, TILE), ((2 * ROW_TILES / (TILE * TILES_DEV)) ** 0.5), 0.5, ((0, 128),)),
        "tile_coords": draw_tile_coords(jax.random.fold_in(arg_keys[12], 71), 0),
        "tile_count": draw_tile_count(jax.random.fold_in(arg_keys[12], 71), 0),
        "boundary_index": place_ends(jax.random.randint(arg_keys[4], (DEVICES, BOUNDARY), 0, ROWS_DEV), jax.random.fold_in(arg_keys[4], 1), 0, ROWS_DEV - 1).astype(jnp.int32),
        "peer_pick": place_ends(jax.random.randint(arg_keys[5], (DEVICES, DEVICES, PEER_ROWS), 0, BOUNDARY), jax.random.fold_in(arg_keys[5], 1), 0, BOUNDARY - 1).astype(jnp.int32),
        "shuffle_order": jax.vmap(lambda own: jax.random.permutation(own, ROWS_DEV))(jax.random.split(arg_keys[6], DEVICES)).reshape((DEVICES, ROWS_DEV)).astype(jnp.int32),
        "attn_weight": scatter_about(arg_keys[7], (LAYERS, 4, WIDTH, WIDTH), WIDTH ** -0.5, 0.25),
        "ffn_in": scatter_about(arg_keys[8], (LAYERS, WIDTH, FFN_HIDDEN), WIDTH ** -0.5, 0.25),
        "ffn_out": scatter_about(arg_keys[9], (LAYERS, FFN_HIDDEN, WIDTH), FFN_HIDDEN ** -0.5, 0.1875),
        "norm_gain": jnp.clip(1.0 + 0.18 * jax.random.normal(arg_keys[10], (LAYERS, 2, WIDTH), jnp.float32), 0.1, 1.9),
        "read_weight": scatter_about(arg_keys[11], (2, WIDTH), (2 * WIDTH) ** -0.5, 0.1875, (), jnp.float32),
    }


def propagate(current, halo_rows, tile_set, tile_place, live_count):
    feat_width = current.shape[1]
    tile_size = tile_set.shape[1]
    row_tiles = current.shape[0] // tile_size
    sources = jnp.concatenate([current, halo_rows], 0).reshape(-1, tile_size, feat_width)
    picked = sources[tile_place[:, 1]]
    product = jnp.einsum('tab,tbf->taf', tile_set.astype(jnp.float32), picked.astype(jnp.float32), precision=lax.Precision.HIGHEST)
    live = (jnp.arange(tile_set.shape[0]) < live_count).astype(jnp.float32)
    selector = (tile_place[:, 0][None, :] == jnp.arange(row_tiles)[:, None]).astype(jnp.float32) * live[None, :]
    summed = jnp.einsum('rt,taf->raf', selector, product, precision=lax.Precision.HIGHEST)
    return summed.reshape(-1, feat_width).astype(jnp.bfloat16)

def layer_norm(inputs, gain):
    center = inputs - lax.optimization_barrier(jnp.mean(inputs, -1, keepdims=True))
    spread = lax.optimization_barrier(jnp.mean(center * center, -1, keepdims=True))
    return center * lax.rsqrt(spread + 1e-05) * gain

def encode(arrived, attn_weight, ffn_in, ffn_out, norm_gain, read_weight):
    node_count = arrived.shape[0]
    token_count = arrived.shape[1]
    feat_width = arrived.shape[2]
    head_dim = feat_width // HEADS
    hidden = arrived.astype(jnp.float32).reshape(node_count * token_count, feat_width)
    for layer_index in range(LAYERS):
        normed = layer_norm(hidden, norm_gain[layer_index, 0]).astype(jnp.bfloat16)
        queries = jnp.dot(normed, attn_weight[layer_index, 0], preferred_element_type=jnp.float32).reshape(node_count, token_count, HEADS, head_dim)
        key_vecs = jnp.dot(normed, attn_weight[layer_index, 1], preferred_element_type=jnp.float32).reshape(node_count, token_count, HEADS, head_dim)
        value_vecs = jnp.dot(normed, attn_weight[layer_index, 2], preferred_element_type=jnp.float32).reshape(node_count, token_count, HEADS, head_dim)
        scores = jnp.einsum('nihd,njhd->nhij', queries, key_vecs, precision=lax.Precision.HIGHEST) * head_dim ** (-0.5)
        weights = jnp.exp(scores)
        weights = weights / lax.optimization_barrier(jnp.sum(weights, -1, keepdims=True))
        context = jnp.einsum('nhij,njhd->nihd', weights, value_vecs, precision=lax.Precision.HIGHEST)
        context = context.reshape(node_count * token_count, feat_width).astype(jnp.bfloat16)
        hidden = hidden + jnp.dot(context, attn_weight[layer_index, 3], preferred_element_type=jnp.float32)
        normed = layer_norm(hidden, norm_gain[layer_index, 1]).astype(jnp.bfloat16)
        expanded = jax.nn.gelu(jnp.dot(normed, ffn_in[layer_index], preferred_element_type=jnp.float32), approximate=True).astype(jnp.bfloat16)
        hidden = hidden + jnp.dot(expanded, ffn_out[layer_index], preferred_element_type=jnp.float32)
    hidden = hidden.reshape(node_count, token_count, feat_width)
    center = hidden[:, 0]
    others = hidden[:, 1:]
    read_score = jnp.dot(center, read_weight[0], precision=lax.Precision.HIGHEST)[:, None] + jnp.einsum('nkf,f->nk', others, read_weight[1], precision=lax.Precision.HIGHEST)
    weights = jnp.exp(read_score)
    weights = weights / lax.optimization_barrier(jnp.sum(weights, -1, keepdims=True))
    return (center + jnp.einsum('nk,nkf->nf', weights, others, precision=lax.Precision.HIGHEST)).astype(jnp.bfloat16)

def pick_rows(block_rows, row_order):
    return block_rows[row_order]

def reference(features, tile_values, tile_coords, tile_count, boundary_index, peer_pick, shuffle_order, attn_weight, ffn_in, ffn_out, norm_gain, read_weight):
    device_count = tile_count.shape[0]
    spread_index = jnp.broadcast_to(boundary_index[:, None, :], (device_count, device_count, BOUNDARY))
    chosen = jnp.take_along_axis(spread_index, peer_pick, axis=2).astype(jnp.int32)
    offsets = (jnp.arange(device_count) * ROWS_DEV).astype(jnp.int32)
    halo_index = (chosen + offsets[:, None, None]).astype(jnp.int32)
    halo_index = jnp.transpose(halo_index, (1, 0, 2)).reshape(device_count, HALO_ROWS)
    current = features
    hop_list = [features]
    for hop_index in range(HOPS):
        flat_rows = current

        def one_device(packed):
            own_rows, halo_at, tile_set, tile_place, live_count = packed
            return propagate(own_rows, flat_rows[halo_at], tile_set, tile_place, live_count)
        current = lax.map(one_device, (current.reshape(device_count, ROWS_DEV, WIDTH), halo_index, tile_values, tile_coords, tile_count)).reshape(NODES, WIDTH)
        hop_list.append(current)
    stacked = jnp.stack(hop_list, 1).reshape(device_count, ROWS_DEV, HOPS + 1, WIDTH)
    shuffled = jax.vmap(pick_rows)(stacked, shuffle_order)
    arrived = shuffled.reshape(N_DOM, N_SHARD, N_SHARD, SHARE, HOPS + 1, WIDTH)
    arrived = jnp.transpose(arrived, (0, 2, 1, 3, 4, 5)).reshape(device_count, ROWS_DEV, HOPS + 1, WIDTH)

    def run_block(block_rows):
        return encode(block_rows, attn_weight, ffn_in, ffn_out, norm_gain, read_weight)
    outcome = lax.map(run_block, arrived)
    return outcome.reshape(NODES, WIDTH)
```

```python
import functools

import jax
import jax.numpy as jnp
from jax import lax
from jax.experimental import pallas as pl
from jax.experimental.pallas import tpu as pltpu
from jax.sharding import PartitionSpec as P

F32, BF16, I32 = jnp.float32, jnp.bfloat16, jnp.int32
MESH = pl.DeviceIdType.MESH
HEADS = 8
HOPS = 4
TOKENS = HOPS + 1
LANES = 128
PARTS = 4
BLOCK = 16
CHUNK = 128
SUB = 32


def dot(a, b):
    return jnp.dot(a, b, preferred_element_type=F32)


def iota(shape, dim):
    return lax.broadcasted_iota(I32, shape, dim)


def onehot(hit):
    return jnp.where(hit, 1.0, 0.0).astype(BF16)


def layer_norm(x, gain):
    center = x - jnp.mean(x, -1, keepdims=True)
    spread = jnp.mean(center * center, -1, keepdims=True)
    return center * lax.rsqrt(spread + 1e-05) * gain


def build_adjacency(coords, count, tiles, out, total):
    size = tiles.shape[2]
    rows, cols = out.shape[0] // size, out.shape[1] // size
    for r in range(rows):
        for c in range(cols):
            total[r, c] = jnp.zeros((size, size), F32)

    def step(t, carry):
        r, c = coords[0, t, 0], coords[0, t, 1]
        total[r, c] += tiles[0, t].astype(F32)
        return carry

    lax.fori_loop(0, count[0], step, 0)
    for r in range(rows):
        for c in range(cols):
            out[r * size : (r + 1) * size, c * size : (c + 1) * size] = total[r, c].astype(BF16)


def window(
    feat,
    adj,
    border,
    picks,
    order,
    attn_any,
    fin_any,
    fout_any,
    gain,
    readw,
    out,
    hops,
    send,
    recv,
    psend,
    own_edge,
    halo_edge,
    adj_own,
    adj_halo,
    halo,
    own,
    q,
    k,
    v,
    attn,
    fin,
    fout,
    pair,
    score,
    ctx,
    hid,
    mid,
    stage,
    send_sem,
    recv_sem,
    weight_sem,
    out_send_sem,
    out_recv_sem,
):
    n_dom, n_shard = lax.axis_size("dom"), lax.axis_size("shard")
    n = n_dom * n_shard
    dom, shard = lax.axis_index("dom"), lax.axis_index("shard")
    me = dom * n_shard + shard
    rows, width = feat.shape

    barrier = pltpu.get_barrier_semaphore()

    def greet(i, carry):
        p = lax.rem(me + i, n)
        pl.semaphore_signal(
            barrier, inc=1, device_id=(p // n_shard, lax.rem(p, n_shard)), device_id_type=MESH
        )
        return carry

    lax.fori_loop(1, n, greet, 0)
    loads = [
        pltpu.make_async_copy(attn_any, attn, weight_sem.at[0]),
        pltpu.make_async_copy(fin_any, fin, weight_sem.at[1]),
        pltpu.make_async_copy(fout_any, fout, weight_sem.at[2]),
    ]
    for load in loads:
        load.start()

    n_pick = picks.shape[2]
    n_edge = border.shape[1]
    pickf = picks[0].astype(F32).astype(BF16)
    lane = iota((n_pick, LANES), 1)
    spread = onehot(lax.rem(lane // n_edge, n_pick) == iota((n_pick, LANES), 0))
    chosen = dot(pickf, spread).astype(I32)
    chosen = onehot(chosen == lax.rem(iota((n, LANES), 1), n_edge))
    for g in range(n * BLOCK // 256):
        shape = (256, n)
        repeat = onehot(iota(shape, 0) // BLOCK + g * (256 // BLOCK) == iota(shape, 1))
        shape = (256, LANES)
        keep = iota(shape, 1) // n_edge == lax.rem(iota(shape, 0), BLOCK)
        psend[g * 256 : (g + 1) * 256, :] = jnp.where(keep, dot(repeat, chosen), 0.0).astype(BF16)

    def edge_of(index_rows):
        at = jnp.zeros((n_edge, rows), I32)
        for b in range(n_edge):
            at = jnp.where(iota((n_edge, rows), 0) == b, border[0, b], at)
        hit = jnp.where(at == index_rows, 1.0, 0.0)
        return jnp.concatenate([hit] * (LANES // n_edge), 0).astype(BF16)

    def diagonal(x):
        step = LANES // PARTS
        return jnp.concatenate(
            [x[c * step : (c + 1) * step, c * LANES : (c + 1) * LANES] for c in range(PARTS)], 0
        )

    def post(r, edge):
        edge = edge.astype(BF16)
        for g in range(n * BLOCK // 256):
            send[r, g * 256 : (g + 1) * 256, :] = dot(psend[g * 256 : (g + 1) * 256, :], edge).astype(BF16)

        def one(i, carry):
            p = lax.rem(me + i * 37, n)
            pltpu.make_async_remote_copy(
                src_ref=send.at[r, pl.ds(pl.multiple_of(p * BLOCK, BLOCK), BLOCK)],
                dst_ref=recv.at[r, pl.ds(pl.multiple_of(me * BLOCK, BLOCK), BLOCK)],
                send_sem=send_sem.at[r],
                recv_sem=recv_sem.at[r],
                device_id=(p // n_shard, lax.rem(p, n_shard)),
                device_id_type=MESH,
            ).start()
            return carry

        lax.fori_loop(1, n, one, 0)
        mine = pl.ds(pl.multiple_of(me * BLOCK, BLOCK), BLOCK)
        pltpu.make_async_copy(send.at[r, mine], recv.at[r, mine], recv_sem.at[r]).start()

    first = diagonal(dot(edge_of(iota((n_edge, rows), 1)), feat[...]))
    pl.semaphore_wait(barrier, n - 1)
    post(0, first)

    place_t = onehot(iota((rows, rows), 0) == order[...])
    place = place_t.astype(F32).T.astype(BF16)
    hops[0] = dot(place, feat[...]).astype(BF16)
    adj_own[...] = dot(dot(place, adj[:, :rows]).astype(BF16), place_t).astype(BF16)
    adj_halo[...] = dot(place, adj[:, rows:]).astype(BF16)
    edge = edge_of(order[...])
    own_edge[...] = dot(edge, adj_own[...]).astype(BF16)
    halo_part = dot(edge, adj_halo[...]).astype(BF16)
    group = LANES // n_pick
    shape = (LANES, LANES * PARTS)
    widen = onehot(
        (iota(shape, 0) // n_pick == iota(shape, 1) // BLOCK)
        & (lax.rem(iota(shape, 0), n_pick) == lax.rem(iota(shape, 1), n_pick))
    )
    shape = (LANES, LANES * PARTS)
    same = iota(shape, 0) // (LANES // PARTS) == lax.rem(iota(shape, 1) // n_pick, PARTS)
    for g in range(n // group):
        wide = dot(halo_part[:, g * LANES : (g + 1) * LANES], widen)
        halo_edge[:, g * LANES * PARTS : (g + 1) * LANES * PARTS] = jnp.where(same, wide, 0.0).astype(BF16)

    def source(i):
        head = lax.rem(i // (LANES // HEADS), HEADS)
        return head * (width // HEADS) + (i // LANES) * (LANES // HEADS) + lax.rem(i, LANES // HEADS)

    shape = (width, width)
    by_row = onehot(iota(shape, 1) == source(iota(shape, 0)))
    by_col = onehot(iota(shape, 0) == source(iota(shape, 1)))
    loads[0].wait()
    for i in range(3):
        attn[0, i] = dot(attn[0, i], by_col).astype(BF16)
    attn[0, 3] = dot(by_row, attn[0, 3]).astype(BF16)

    per = 256 // BLOCK
    shape = (256, 256)
    row, col = iota(shape, 0), iota(shape, 1)
    regroup = onehot(
        (lax.rem(row // n_pick, per) == col // BLOCK)
        & (row // (256 // PARTS) == lax.rem(col // n_pick, PARTS))
        & (lax.rem(row, n_pick) == lax.rem(col, n_pick))
    )

    def project(h):
        def part(b, carry):
            at = pl.ds(pl.multiple_of(b * 256, 256), 256)
            a = layer_norm(hops[h, at, :].astype(F32), gain[0, 0:1, :]).astype(BF16)
            q[h, at, :] = dot(a, attn[0, 0])
            k[h, at, :] = dot(a, attn[0, 1])
            v[h, at, :] = dot(a, attn[0, 2])
            return carry

        lax.fori_loop(0, rows // 256, part, 0)

    def hop(r, carry):
        x = hops[r]
        own_part = diagonal(dot(own_edge[...], x))
        own[...] = dot(adj_own[...], x)
        project(r)
        pltpu.make_async_copy(recv.at[r], recv.at[r], recv_sem.at[r]).wait()

        @pl.when(r < HOPS - 1)
        def _():
            post(r + 1, own_part + dot(halo_edge[...], recv[r]))

        span = 256 // PARTS
        for g in range(n * BLOCK // 512):
            both = jnp.concatenate(
                [recv[r, g * 512 : g * 512 + 256, :], recv[r, g * 512 + 256 : (g + 1) * 512, :]], 1
            )
            moved = dot(regroup, both).astype(BF16)
            for c in range(PARTS):
                for d in range(2):
                    halo[(2 * g + d) * span : (2 * g + d + 1) * span, c * LANES : (c + 1) * LANES] = moved[
                        c * span : (c + 1) * span, d * LANES : (d + 1) * LANES
                    ]
        hops[r + 1] = (own[...] + dot(adj_halo[...], halo[...])).astype(BF16)
        return carry

    lax.fori_loop(0, HOPS, hop, 0)
    project(HOPS)
    loads[1].wait()
    loads[2].wait()

    shape = (2 * LANES, LANES)
    seg = LANES // HEADS
    gather = jnp.where(
        lax.rem(iota(shape, 0), LANES) // seg == iota(shape, 1) // seg, (width // HEADS) ** -0.5, 0.0
    ).astype(BF16)
    share = rows // n_shard
    n_chunk = rows // CHUNK

    def lanes(c):
        return slice(c * LANES, (c + 1) * LANES)

    def layer(step, carry):
        at_chunk = lax.rem(step + shard // (n_shard // n_chunk), n_chunk)
        base = at_chunk * CHUNK

        def scores(b, carry):
            at = pl.ds(pl.multiple_of(base + b * SUB, SUB), SUB)
            for i in range(TOKENS):
                qs = [q[i, at, lanes(c)] for c in range(PARTS)]
                for j in range(TOKENS):
                    s = qs[0] * k[j, at, lanes(0)]
                    for c in range(1, PARTS):
                        s += qs[c] * k[j, at, lanes(c)]
                    high = s.astype(BF16)
                    low = (s - high.astype(F32)).astype(BF16)
                    to = pl.ds(pl.multiple_of((i * TOKENS + j) * CHUNK + b * SUB, SUB), SUB)
                    pair[to, lanes(0)] = high
                    pair[to, lanes(1)] = low
            return carry

        lax.fori_loop(0, CHUNK // SUB, scores, 0)
        score[...] = dot(pair[...], gather)

        def mix(b, carry):
            at = pl.ds(pl.multiple_of(base + b * SUB, SUB), SUB)
            for i in range(TOKENS):
                s = [
                    score[pl.ds(pl.multiple_of((i * TOKENS + j) * CHUNK + b * SUB, SUB), SUB), :]
                    for j in range(TOKENS)
                ]
                top = functools.reduce(jnp.maximum, s)
                e = [jnp.exp(x - top) for x in s]
                scale = 1.0 / functools.reduce(jnp.add, e)
                w = [x * scale for x in e]
                to = pl.ds(pl.multiple_of(i * CHUNK + b * SUB, SUB), SUB)
                for c in range(PARTS):
                    total = w[0] * v[0, at, lanes(c)]
                    for j in range(1, TOKENS):
                        total += w[j] * v[j, at, lanes(c)]
                    ctx[to, lanes(c)] = total.astype(BF16)
            return carry

        lax.fori_loop(0, CHUNK // SUB, mix, 0)
        at = pl.ds(pl.multiple_of(base, CHUNK), CHUNK)
        hid[...] = dot(ctx[...], attn[0, 3])
        for i in range(TOKENS):
            to = slice(i * CHUNK, (i + 1) * CHUNK)
            h = hops[i, at, :].astype(F32) + hid[to, :]
            hid[to, :] = h
            ctx[to, :] = layer_norm(h, gain[0, 1:2, :]).astype(BF16)
        for b in range(mid.shape[1] // 256):
            x = dot(ctx[...], fin[0, :, b * 256 : (b + 1) * 256])
            mid[:, b * 256 : (b + 1) * 256] = jax.nn.gelu(x, approximate=True).astype(BF16)
        hid[...] += dot(mid[...], fout[0])

        z0 = hid[0:CHUNK, :]
        base_score = jnp.sum(z0 * readw[0:1, :], -1, keepdims=True)
        s = [
            base_score + jnp.sum(hid[i * CHUNK : (i + 1) * CHUNK, :] * readw[1:2, :], -1, keepdims=True)
            for i in range(1, TOKENS)
        ]
        top = functools.reduce(jnp.maximum, s)
        e = [jnp.exp(x - top) for x in s]
        scale = 1.0 / functools.reduce(jnp.add, e)
        state = z0
        for i in range(1, TOKENS):
            state += (e[i - 1] * scale) * hid[i * CHUNK : (i + 1) * CHUNK, :]
        stage[at, :] = state.astype(BF16)

        def deal(t, carry):
            to = at_chunk * (CHUNK // share) + t
            src = stage.at[pl.ds(pl.multiple_of(to * share, share), share)]
            dst = out.at[pl.ds(pl.multiple_of(shard * share, share), share)]

            @pl.when(to != shard)
            def _():
                pltpu.make_async_remote_copy(
                    src_ref=src,
                    dst_ref=dst,
                    send_sem=out_send_sem,
                    recv_sem=out_recv_sem,
                    device_id=(dom, to),
                    device_id_type=MESH,
                ).start()

            @pl.when(to == shard)
            def _():
                pltpu.make_async_copy(src, dst, out_recv_sem).start()

            return carry

        lax.fori_loop(0, CHUNK // share, deal, 0)
        return carry

    lax.fori_loop(0, n_chunk, layer, 0)

    sent = send.at[0, pl.ds(0, (n - 1) * BLOCK)]
    for r in range(HOPS):
        pltpu.make_async_copy(sent, sent, send_sem.at[r]).wait()
    sent = stage.at[pl.ds(0, rows - share)]
    pltpu.make_async_copy(sent, sent, out_send_sem).wait()
    pltpu.make_async_copy(out, out, out_recv_sem).wait()


def local(
    features,
    tile_values,
    tile_coords,
    tile_count,
    boundary_index,
    peer_pick,
    shuffle_order,
    attn_weight,
    ffn_in,
    ffn_out,
    norm_gain,
    read_weight,
):
    rows, width = features.shape
    size = tile_values.shape[2]
    n, n_pick = peer_pick.shape[1], peer_pick.shape[2]
    halo_rows = n * n_pick
    hidden = ffn_in.shape[2]
    vmem = pl.BlockSpec(memory_space=pltpu.VMEM)
    smem = pl.BlockSpec(memory_space=pltpu.SMEM)
    hbm = pl.BlockSpec(memory_space=pl.ANY)
    adj = pl.pallas_call(
        build_adjacency,
        out_shape=jax.ShapeDtypeStruct((rows, rows + halo_rows), BF16),
        in_specs=[smem, smem, vmem],
        out_specs=vmem,
        scratch_shapes=[pltpu.VMEM((8, 8, size, size), F32)],
        compiler_params=pltpu.CompilerParams(vmem_limit_bytes=24 * 2**20),
        name="adjacency",
    )(tile_coords, tile_count, tile_values)
    message = n * BLOCK
    return pl.pallas_call(
        window,
        out_shape=jax.ShapeDtypeStruct((rows, width), BF16),
        in_specs=[vmem, vmem, smem, vmem, vmem, hbm, hbm, hbm, vmem, vmem],
        out_specs=vmem,
        scratch_shapes=[
            pltpu.VMEM((TOKENS, rows, width), BF16),
            pltpu.VMEM((HOPS, message, LANES), BF16),
            pltpu.VMEM((HOPS, message, LANES), BF16),
            pltpu.VMEM((message, LANES), BF16),
            pltpu.VMEM((LANES, rows), BF16),
            pltpu.VMEM((LANES, message), BF16),
            pltpu.VMEM((rows, rows), BF16),
            pltpu.VMEM((rows, halo_rows), BF16),
            pltpu.VMEM((halo_rows, width), BF16),
            pltpu.VMEM((rows, width), F32),
            pltpu.VMEM((TOKENS, rows, width), F32),
            pltpu.VMEM((TOKENS, rows, width), F32),
            pltpu.VMEM((TOKENS, rows, width), F32),
            pltpu.VMEM(attn_weight.shape, BF16),
            pltpu.VMEM(ffn_in.shape, BF16),
            pltpu.VMEM(ffn_out.shape, BF16),
            pltpu.VMEM((TOKENS * TOKENS * CHUNK, 2 * LANES), BF16),
            pltpu.VMEM((TOKENS * TOKENS * CHUNK, LANES), F32),
            pltpu.VMEM((TOKENS * CHUNK, width), BF16),
            pltpu.VMEM((TOKENS * CHUNK, width), F32),
            pltpu.VMEM((TOKENS * CHUNK, hidden), BF16),
            pltpu.VMEM((rows, width), BF16),
            pltpu.SemaphoreType.DMA((HOPS,)),
            pltpu.SemaphoreType.DMA((HOPS,)),
            pltpu.SemaphoreType.DMA((3,)),
            pltpu.SemaphoreType.DMA,
            pltpu.SemaphoreType.DMA,
        ],
        compiler_params=pltpu.CompilerParams(
            collective_id=0, has_side_effects=True, vmem_limit_bytes=56 * 2**20
        ),
        name="window",
    )(
        features,
        adj,
        boundary_index,
        peer_pick,
        shuffle_order,
        attn_weight,
        ffn_in,
        ffn_out,
        norm_gain,
        read_weight,
    )


def solution(mesh):
    placed = (
        P(("dom", "shard"), None),
        P(("dom", "shard"), None, None, None),
        P(("dom", "shard"), None, None),
        P(("dom", "shard")),
        P(("dom", "shard"), None),
        P(("dom", "shard"), None, None),
        P(("dom", "shard"), None),
        P(),
        P(),
        P(),
        P(),
        P(),
    )
    return jax.shard_map(
        local, mesh=mesh, in_specs=placed, out_specs=P(("dom", "shard"), None), check_vma=False
    )
```

```python
import functools

import jax
import jax.numpy as jnp
from jax import lax
from jax.experimental import pallas as pl
from jax.experimental.pallas import tpu as pltpu
from jax.sharding import PartitionSpec as P

F32, BF16, I32 = jnp.float32, jnp.bfloat16, jnp.int32
MESH = pl.DeviceIdType.MESH
SIDE = 4
HEADS = 8
HOPS = 4
TOKENS = HOPS + 1
LANES = 128
PARTS = 4
HALVES = 2
EACH = PARTS // HALVES
BLOCK = 8
CHUNK = 128
SUB = 32


def dot(a, b):
    return jnp.dot(a, b, preferred_element_type=F32)


def iota(shape, dim):
    return lax.broadcasted_iota(I32, shape, dim)


def onehot(hit):
    return jnp.where(hit, 1.0, 0.0).astype(BF16)


def layer_norm(x, gain):
    center = x - jnp.mean(x, -1, keepdims=True)
    spread = jnp.mean(center * center, -1, keepdims=True)
    return center * lax.rsqrt(spread + 1e-05) * gain


def window(
    feat,
    coords,
    count,
    border,
    picks,
    order,
    tiles_any,
    attn_any,
    fin_any,
    fout_any,
    gain,
    readw,
    out,
    hops,
    send,
    recv,
    psend,
    own_edge,
    halo_edge,
    adj_own,
    adj_halo,
    halo,
    own,
    own_diag,
    q,
    k,
    v,
    attn,
    fin,
    fout,
    tiles,
    total,
    link,
    link_at,
    adj,
    score,
    ctx,
    norm,
    hid,
    mid,
    stage,
    send_sem,
    recv_sem,
    load_sem,
    link_sem,
    out_send_sem,
    out_recv_sem,
):
    n_dom, n_shard = lax.axis_size("dom"), lax.axis_size("shard")
    n = n_dom * n_shard
    dom, shard = lax.axis_index("dom"), lax.axis_index("shard")
    me = dom * n_shard + shard
    rows, width = feat.shape

    barrier = pltpu.get_barrier_semaphore()

    ring = range(SIDE)
    doms = {
        (dz, dc): lax.rem(dom // 2 + dz, SIDE) * 2 + lax.rem(dom + dc, 2) for dz in ring for dc in range(2)
    }
    shards = {
        (dy, dx): lax.rem(shard // SIDE + dy, SIDE) * SIDE + lax.rem(shard + dx, SIDE)
        for dy in ring
        for dx in ring
    }

    def away(at):
        return sum(min(d, SIDE - d) for d in (at[0][0], *at[1]))

    partners = [(a, b) for a in doms for b in shards if (a, b) != ((0, 0), (0, 0))]
    partners = [(doms[a], shards[b]) for a, b in sorted(partners, key=away, reverse=True)]
    for p in partners:
        pl.semaphore_signal(barrier, inc=1, device_id=p, device_id_type=MESH)
    loads = [
        pltpu.make_async_copy(src, dst, load_sem.at[i])
        for i, (src, dst) in enumerate(
            [(tiles_any, tiles), (attn_any, attn), (fin_any, fin), (fout_any, fout)]
        )
    ]
    for load in loads:
        load.start()

    n_pick = picks.shape[1]
    n_edge = border.shape[1]
    pickf = picks[0].astype(F32).astype(BF16)
    span = BLOCK * n_edge
    lane = iota((n_pick, span), 1)
    spread = onehot(lax.rem(lane // n_edge, n_pick) == iota((n_pick, span), 0))
    chosen = lax.dot_general(
        pickf, spread, (((0,), (0,)), ((), ())), preferred_element_type=F32
    ).astype(I32)
    chosen = onehot(chosen == lax.rem(iota((n, span), 1), n_edge))
    for g in range(n * BLOCK // 256):
        shape = (256, n)
        repeat = onehot(iota(shape, 0) // BLOCK + g * (256 // BLOCK) == iota(shape, 1))
        shape = (256, span)
        keep = iota(shape, 1) // n_edge == lax.rem(iota(shape, 0), BLOCK)
        psend[g * 256 : (g + 1) * 256, :] = jnp.where(keep, dot(repeat, chosen), 0.0).astype(BF16)

    slots, size = tiles.shape[1], tiles.shape[2]
    row_tiles, col_tiles = adj.shape[0] // size, adj.shape[1] // size
    at = coords[0, 0:1, :] * col_tiles + coords[0, 1:2, :]
    lane = iota((1, slots), 1)
    at = jnp.where(lane < count[0, 0], at, col_tiles * col_tiles + lane).astype(F32)
    shape = (slots, slots)
    row, col = iota(shape, 0), iota(shape, 1)
    at_col = jnp.sum(jnp.where(row == col, at, 0.0), 1, keepdims=True)
    slot = (row + 1).astype(F32)
    before = jnp.max(jnp.where((at_col == at) & (row < col), slot, 0.0), 0, keepdims=True)
    final = jnp.max(jnp.where(at_col == col.astype(F32), slot, 0.0), 0, keepdims=True)
    link[...] = jnp.zeros(link.shape, I32)
    link[0:1, 0:slots] = before.astype(I32)
    link[1:2, 0:slots] = final.astype(I32)
    to_scalars = pltpu.make_async_copy(link, link_at, link_sem)
    to_scalars.start()

    def edge_of(index_rows):
        at = jnp.zeros((n_edge, rows), I32)
        for b in range(n_edge):
            at = jnp.where(iota((n_edge, rows), 0) == b, border[0, b], at)
        hit = jnp.where(at == index_rows, 1.0, 0.0)
        return jnp.concatenate([hit] * (span // n_edge), 0).astype(BF16)

    def diagonal(x, f):
        step = span // EACH
        return jnp.concatenate(
            [
                x[c * step : (c + 1) * step, (f * EACH + c) * LANES : (f * EACH + c + 1) * LANES]
                for c in range(EACH)
            ],
            0,
        )

    def post(r, f, edge):
        edge = edge.astype(BF16)
        for g in range(n * BLOCK // 256):
            block = dot(psend[g * 256 : (g + 1) * 256, :], edge)
            send[r, f, g * (256 // BLOCK) : (g + 1) * (256 // BLOCK)] = block.reshape(
                256 // BLOCK, BLOCK, LANES
            ).astype(BF16)

        for p in partners:
            pltpu.make_async_remote_copy(
                src_ref=send.at[r, f, p[0] * n_shard + p[1]],
                dst_ref=recv.at[r, f, me],
                send_sem=send_sem.at[r, f],
                recv_sem=recv_sem.at[r, f],
                device_id=p,
                device_id_type=MESH,
            ).start()
        pltpu.make_async_copy(send.at[r, f, me], recv.at[r, f, me], recv_sem.at[r, f]).start()

    first = dot(edge_of(iota((n_edge, rows), 1)), feat[...])
    pl.semaphore_wait(barrier, n - 1)
    for f in range(HALVES):
        post(0, f, diagonal(first, f))

    to_scalars.wait()
    loads[0].wait()
    total[0] = jnp.zeros((size, size), F32)

    def gather_slot(t, carry):
        total[t + 1] = total[jnp.clip(link_at[0, t], 0, slots)] + tiles[0, t].astype(F32)
        return carry

    lax.fori_loop(0, slots, gather_slot, 0)
    for r in range(row_tiles):
        for c in range(col_tiles):
            adj[r * size : (r + 1) * size, c * size : (c + 1) * size] = total[
                jnp.clip(link_at[1, r * col_tiles + c], 0, slots)
            ].astype(BF16)

    place_t = onehot(iota((rows, rows), 0) == order[...])
    place = place_t.astype(F32).T.astype(BF16)
    hops[0] = dot(place, feat[...]).astype(BF16)
    adj_own[...] = dot(dot(place, adj[:, :rows]).astype(BF16), place_t).astype(BF16)
    adj_halo[...] = dot(place, adj[:, rows:]).astype(BF16)
    edge = edge_of(order[...])
    own_edge[...] = dot(edge, adj_own[...]).astype(BF16)
    halo_part = dot(edge, adj_halo[...]).astype(BF16)
    group = LANES // n_pick
    shape = (LANES, LANES * EACH)
    widen = onehot(
        (iota(shape, 0) // n_pick == iota(shape, 1) // BLOCK)
        & (lax.rem(iota(shape, 0), n_pick) == lax.rem(iota(shape, 1), n_pick))
    )
    shape = (span, LANES * EACH)
    same = iota(shape, 0) // (span // EACH) == lax.rem(iota(shape, 1) // n_pick, EACH)
    for g in range(n // group):
        wide = dot(halo_part[:, g * LANES : (g + 1) * LANES], widen)
        halo_edge[:, g * LANES * EACH : (g + 1) * LANES * EACH] = jnp.where(same, wide, 0.0).astype(BF16)

    def source(i):
        head = lax.rem(i // (LANES // HEADS), HEADS)
        return head * (width // HEADS) + (i // LANES) * (LANES // HEADS) + lax.rem(i, LANES // HEADS)

    shape = (width, width)
    by_row = onehot(iota(shape, 1) == source(iota(shape, 0)))
    by_col = onehot(iota(shape, 0) == source(iota(shape, 1)))
    loads[1].wait()
    for i in range(3):
        attn[0, i] = dot(attn[0, i], by_col).astype(BF16)
    attn[0, 3] = dot(by_row, attn[0, 3]).astype(BF16)

    per = 256 // BLOCK
    shape = (256, 256)
    row, col = iota(shape, 0), iota(shape, 1)
    regroup = onehot(
        (lax.rem(row // n_pick, per) == col // BLOCK)
        & (row // (256 // EACH) == lax.rem(col // n_pick, EACH))
        & (lax.rem(row, n_pick) == lax.rem(col, n_pick))
    )

    shape = (2 * LANES, 2 * LANES)
    seg = LANES // HEADS
    gather = jnp.where(
        iota(shape, 0) // seg == iota(shape, 1) // seg, (width // HEADS) ** -0.5, 0.0
    ).astype(BF16)

    def lanes(c):
        return slice(c * LANES, (c + 1) * LANES)

    def project(h):
        for b in range(rows // 256):
            at = slice(b * 256, (b + 1) * 256)
            a = layer_norm(hops[h, at, :].astype(F32), gain[0, 0:1, :]).astype(BF16)
            q[h, at, :] = dot(a, attn[0, 0]).astype(BF16)
            k[h, at, :] = dot(a, attn[0, 1]).astype(BF16)
            v[h, at, :] = dot(a, attn[0, 2])

        def against(j, carry):
            for b in range(rows // CHUNK):
                at = slice(b * CHUNK, (b + 1) * CHUNK)

                def product(x, y):
                    p = [q[x, at, lanes(c)] * k[y, at, lanes(c)] for c in range(PARTS)]
                    return (p[0] + p[1]) + (p[2] + p[3])

                score[h, j, at, :] = dot(jnp.concatenate([product(h, j), product(j, h)], 1), gather)
            return carry

        lax.fori_loop(0, h + 1, against, 0)

    def arrived(r, f):
        pltpu.make_async_copy(recv.at[r, f], recv.at[r, f], recv_sem.at[r, f]).wait()
        return recv[r, f].astype(F32).reshape(n * BLOCK, LANES).astype(BF16)

    def advance(r, f, got):
        part = 256 // EACH
        for g in range(n * BLOCK // 512):
            both = jnp.concatenate([got[g * 512 : g * 512 + 256], got[g * 512 + 256 : (g + 1) * 512]], 1)
            moved = dot(regroup, both).astype(BF16)
            for c in range(EACH):
                for d in range(2):
                    halo[f, (2 * g + d) * part : (2 * g + d + 1) * part, lanes(c)] = moved[
                        c * part : (c + 1) * part, lanes(d)
                    ]
        at = slice(f * EACH * LANES, (f + 1) * EACH * LANES)
        hops[r + 1, :, at] = (own[:, at] + dot(adj_halo[...], halo[f])).astype(BF16)

    def prepare(r):
        own[...] = dot(adj_own[...], hops[r])
        project(r)

    def hop(r, carry):
        own_part = dot(own_edge[...], hops[r])
        for f in range(HALVES):
            own_diag[f] = diagonal(own_part, f)
        prepare(r)
        for f in range(HALVES):
            got = arrived(r, f)
            post(r + 1, f, own_diag[f] + dot(halo_edge[...], got))
            advance(r, f, got)
        return carry

    lax.fori_loop(0, HOPS - 1, hop, 0)
    prepare(HOPS - 1)
    for f in range(HALVES):
        advance(HOPS - 1, f, arrived(HOPS - 1, f))
    project(HOPS)
    loads[2].wait()
    loads[3].wait()

    share = rows // n_shard
    n_chunk = rows // CHUNK
    side = CHUNK // share

    def chunk_at(step):
        return lax.rem(shard // side + (2, 3, 1, 0)[step], n_chunk)

    def mix(step):
        base = chunk_at(step) * CHUNK
        for b in range(CHUNK // SUB):
            at = pl.ds(pl.multiple_of(base + b * SUB, SUB), SUB)
            for i in range(TOKENS):
                s = [
                    score[max(i, j), min(i, j), at, lanes(0 if i >= j else 1)]
                    for j in range(TOKENS)
                ]
                top = functools.reduce(jnp.maximum, s)
                e = [jnp.exp(x - top) for x in s]
                scale = 1.0 / functools.reduce(jnp.add, e)
                w = [x * scale for x in e]
                to = slice(i * CHUNK + b * SUB, i * CHUNK + (b + 1) * SUB)
                for c in range(PARTS):
                    acc = w[0] * v[0, at, lanes(c)]
                    for j in range(1, TOKENS):
                        acc += w[j] * v[j, at, lanes(c)]
                    ctx[step % 2, to, lanes(c)] = acc.astype(BF16)

    def layer(step):
        at_chunk = chunk_at(step)
        base = at_chunk * CHUNK
        at = pl.ds(pl.multiple_of(base, CHUNK), CHUNK)
        if step + 1 < n_chunk:
            mix(step + 1)
        two = step % 2
        hid[two] = dot(ctx[two], attn[0, 3])
        for i in range(TOKENS):
            to = slice(i * CHUNK, (i + 1) * CHUNK)
            h = hops[i, at, :].astype(F32) + hid[two, to, :]
            hid[two, to, :] = h
            norm[two, to, :] = layer_norm(h, gain[0, 1:2, :]).astype(BF16)
        for b in range(mid.shape[2] // 256):
            x = dot(norm[two], fin[0, :, b * 256 : (b + 1) * 256])
            mid[two, :, b * 256 : (b + 1) * 256] = jax.nn.gelu(x, approximate=True).astype(BF16)
        hid[two] += dot(mid[two], fout[0])

        z0 = hid[two, 0:CHUNK, :]
        base_score = jnp.sum(z0 * readw[0:1, :], -1, keepdims=True)
        s = [
            base_score + jnp.sum(hid[two, i * CHUNK : (i + 1) * CHUNK, :] * readw[1:2, :], -1, keepdims=True)
            for i in range(1, TOKENS)
        ]
        top = functools.reduce(jnp.maximum, s)
        e = [jnp.exp(x - top) for x in s]
        scale = 1.0 / functools.reduce(jnp.add, e)
        state = z0
        for i in range(1, TOKENS):
            state += (e[i - 1] * scale) * hid[two, i * CHUNK : (i + 1) * CHUNK, :]
        stage[at, :] = state.astype(BF16)

        dst = out.at[pl.ds(pl.multiple_of(shard * share, share), share)]
        for far in (2, 3, 1, 0):
            to = at_chunk * side + lax.rem(lax.rem(shard, side) + far, side)
            src = stage.at[pl.ds(pl.multiple_of(to * share, share), share)]
            if step == n_chunk - 1 and far == 0:
                pltpu.make_async_copy(src, dst, out_recv_sem).start()
            else:
                pltpu.make_async_remote_copy(
                    src_ref=src,
                    dst_ref=dst,
                    send_sem=out_send_sem,
                    recv_sem=out_recv_sem,
                    device_id=(dom, to),
                    device_id_type=MESH,
                ).start()

    mix(0)
    for step in range(n_chunk):
        layer(step)

    sent = send.at[0, 0, pl.ds(0, n - 1)]
    for r in range(HOPS):
        for f in range(HALVES):
            pltpu.make_async_copy(sent, sent, send_sem.at[r, f]).wait()
    sent = stage.at[pl.ds(0, rows - share)]
    pltpu.make_async_copy(sent, sent, out_send_sem).wait()
    pltpu.make_async_copy(out, out, out_recv_sem).wait()


def local(
    features,
    tile_values,
    tile_coords,
    tile_count,
    boundary_index,
    peer_pick,
    shuffle_order,
    attn_weight,
    ffn_in,
    ffn_out,
    norm_gain,
    read_weight,
):
    rows, width = features.shape
    size = tile_values.shape[2]
    n, n_pick = peer_pick.shape[1], peer_pick.shape[2]
    halo_rows = n * n_pick
    hidden = ffn_in.shape[2]
    vmem = pl.BlockSpec(memory_space=pltpu.VMEM)
    smem = pl.BlockSpec(memory_space=pltpu.SMEM)
    hbm = pl.BlockSpec(memory_space=pl.ANY)
    message = n * BLOCK
    span = BLOCK * boundary_index.shape[1]
    states = pl.pallas_call(
        window,
        out_shape=jax.ShapeDtypeStruct((rows, width), BF16),
        in_specs=[vmem, vmem, smem, smem, vmem, vmem, hbm, hbm, hbm, hbm, vmem, vmem],
        out_specs=hbm,
        scratch_shapes=[
            pltpu.VMEM((TOKENS, rows, width), BF16),
            pltpu.VMEM((HOPS, HALVES, n, BLOCK, LANES), BF16),
            pltpu.VMEM((HOPS, HALVES, n, BLOCK, LANES), BF16),
            pltpu.VMEM((message, span), BF16),
            pltpu.VMEM((span, rows), BF16),
            pltpu.VMEM((span, message), BF16),
            pltpu.VMEM((rows, rows), BF16),
            pltpu.VMEM((rows, halo_rows), BF16),
            pltpu.VMEM((HALVES, halo_rows, EACH * LANES), BF16),
            pltpu.VMEM((rows, width), F32),
            pltpu.VMEM((HALVES, span, LANES), F32),
            pltpu.VMEM((TOKENS, rows, width), BF16),
            pltpu.VMEM((TOKENS, rows, width), BF16),
            pltpu.VMEM((TOKENS, rows, width), F32),
            pltpu.VMEM(attn_weight.shape, BF16),
            pltpu.VMEM(ffn_in.shape, BF16),
            pltpu.VMEM(ffn_out.shape, BF16),
            pltpu.VMEM(tile_values.shape, BF16),
            pltpu.VMEM((tile_values.shape[1] + 1, size, size), F32),
            pltpu.VMEM((8, LANES), I32),
            pltpu.SMEM((8, LANES), I32),
            pltpu.VMEM((rows, rows + halo_rows), BF16),
            pltpu.VMEM((TOKENS, TOKENS, rows, 2 * LANES), F32),
            pltpu.VMEM((2, TOKENS * CHUNK, width), BF16),
            pltpu.VMEM((2, TOKENS * CHUNK, width), BF16),
            pltpu.VMEM((2, TOKENS * CHUNK, width), F32),
            pltpu.VMEM((2, TOKENS * CHUNK, hidden), BF16),
            pltpu.VMEM((rows, width), BF16),
            pltpu.SemaphoreType.DMA((HOPS, HALVES)),
            pltpu.SemaphoreType.DMA((HOPS, HALVES)),
            pltpu.SemaphoreType.DMA((4,)),
            pltpu.SemaphoreType.DMA,
            pltpu.SemaphoreType.DMA,
            pltpu.SemaphoreType.DMA,
        ],
        compiler_params=pltpu.CompilerParams(
            collective_id=0, has_side_effects=True, vmem_limit_bytes=56 * 2**20
        ),
        name="window",
    )(
        features,
        jnp.swapaxes(tile_coords, 1, 2),
        tile_count.reshape(1, 1),
        boundary_index,
        jnp.swapaxes(peer_pick, 1, 2),
        shuffle_order,
        tile_values,
        attn_weight,
        ffn_in,
        ffn_out,
        norm_gain,
        read_weight,
    )
    return states


def solution(mesh):
    placed = (
        P(("dom", "shard"), None),
        P(("dom", "shard"), None, None, None),
        P(("dom", "shard"), None, None),
        P(("dom", "shard")),
        P(("dom", "shard"), None),
        P(("dom", "shard"), None, None),
        P(("dom", "shard"), None),
        P(),
        P(),
        P(),
        P(),
        P(),
    )
    return jax.shard_map(
        local, mesh=mesh, in_specs=placed, out_specs=P(("dom", "shard"), None), check_vma=False
    )
```

```python
import functools

import jax
import jax.numpy as jnp
from jax import lax
from jax.experimental import pallas as pl
from jax.experimental.pallas import tpu as pltpu
from jax.sharding import PartitionSpec as P

F32, BF16, I32 = jnp.float32, jnp.bfloat16, jnp.int32
MESH = pl.DeviceIdType.MESH
SIDE = 4
HEADS = 8
HOPS = 4
TOKENS = HOPS + 1
LANES = 128
PARTS = 4
HALVES = 2
EACH = PARTS // HALVES
BLOCK = 8
CHUNK = 128
SUB = 32


def dot(a, b):
    return jnp.dot(a, b, preferred_element_type=F32)


def iota(shape, dim):
    return lax.broadcasted_iota(I32, shape, dim)


def onehot(hit):
    return jnp.where(hit, 1.0, 0.0).astype(BF16)


def layer_norm(x, gain):
    center = x - jnp.mean(x, -1, keepdims=True)
    spread = jnp.mean(center * center, -1, keepdims=True)
    return center * lax.rsqrt(spread + 1e-05) * gain


def window(
    feat,
    coords,
    count,
    border,
    picks,
    order,
    tiles_any,
    attn_any,
    fin_any,
    fout_any,
    gain,
    readw,
    out,
    hops,
    send,
    recv,
    psend,
    own_edge,
    halo_edge,
    adj_own,
    adj_halo,
    halo,
    own,
    own_diag,
    q,
    k,
    v,
    attn,
    fin,
    fout,
    tiles,
    total,
    link,
    link_at,
    adj,
    score,
    ctx,
    norm,
    hid,
    mid,
    stage,
    send_sem,
    recv_sem,
    load_sem,
    link_sem,
    out_send_sem,
    out_recv_sem,
):
    n_dom, n_shard = lax.axis_size("dom"), lax.axis_size("shard")
    n = n_dom * n_shard
    dom, shard = lax.axis_index("dom"), lax.axis_index("shard")
    me = dom * n_shard + shard
    rows, width = feat.shape

    barrier = pltpu.get_barrier_semaphore()

    ring = range(SIDE)
    doms = {
        (dz, dc): lax.rem(dom // 2 + dz, SIDE) * 2 + lax.rem(dom + dc, 2) for dz in ring for dc in range(2)
    }
    shards = {
        (dy, dx): lax.rem(shard // SIDE + dy, SIDE) * SIDE + lax.rem(shard + dx, SIDE)
        for dy in ring
        for dx in ring
    }

    def away(at):
        return sum(min(d, SIDE - d) for d in (at[0][0], *at[1]))

    partners = [(a, b) for a in doms for b in shards if (a, b) != ((0, 0), (0, 0))]
    partners = [(doms[a], shards[b]) for a, b in sorted(partners, key=away, reverse=True)]
    for p in partners:
        pl.semaphore_signal(barrier, inc=1, device_id=p, device_id_type=MESH)
    loads = [
        pltpu.make_async_copy(src, dst, load_sem.at[i])
        for i, (src, dst) in enumerate(
            [(tiles_any, tiles), (attn_any, attn), (fin_any, fin), (fout_any, fout)]
        )
    ]
    for load in loads:
        load.start()

    n_pick = picks.shape[1]
    n_edge = border.shape[1]
    pickf = picks[0].astype(F32).astype(BF16)
    span = BLOCK * n_edge
    lane = iota((n_pick, span), 1)
    spread = onehot(lax.rem(lane // n_edge, n_pick) == iota((n_pick, span), 0))
    chosen = lax.dot_general(
        pickf, spread, (((0,), (0,)), ((), ())), preferred_element_type=F32
    ).astype(I32)
    chosen = onehot(chosen == lax.rem(iota((n, span), 1), n_edge))
    for g in range(n * BLOCK // 256):
        shape = (256, n)
        repeat = onehot(iota(shape, 0) // BLOCK + g * (256 // BLOCK) == iota(shape, 1))
        shape = (256, span)
        keep = iota(shape, 1) // n_edge == lax.rem(iota(shape, 0), BLOCK)
        psend[g * 256 : (g + 1) * 256, :] = jnp.where(keep, dot(repeat, chosen), 0.0).astype(BF16)

    slots, size = tiles.shape[1], tiles.shape[2]
    row_tiles, col_tiles = adj.shape[0] // size, adj.shape[1] // size
    at = coords[0, 0:1, :] * col_tiles + coords[0, 1:2, :]
    lane = iota((1, slots), 1)
    at = jnp.where(lane < count[0, 0], at, col_tiles * col_tiles + lane).astype(F32)
    shape = (slots, slots)
    row, col = iota(shape, 0), iota(shape, 1)
    at_col = jnp.sum(jnp.where(row == col, at, 0.0), 1, keepdims=True)
    slot = (row + 1).astype(F32)
    before = jnp.max(jnp.where((at_col == at) & (row < col), slot, 0.0), 0, keepdims=True)
    final = jnp.max(jnp.where(at_col == col.astype(F32), slot, 0.0), 0, keepdims=True)
    link[...] = jnp.zeros(link.shape, I32)
    link[0:1, 0:slots] = before.astype(I32)
    link[1:2, 0:slots] = final.astype(I32)
    to_scalars = pltpu.make_async_copy(link, link_at, link_sem)
    to_scalars.start()

    def edge_of(index_rows):
        at = jnp.zeros((n_edge, rows), I32)
        for b in range(n_edge):
            at = jnp.where(iota((n_edge, rows), 0) == b, border[0, b], at)
        hit = jnp.where(at == index_rows, 1.0, 0.0)
        return jnp.concatenate([hit] * (span // n_edge), 0).astype(BF16)

    def diagonal(x, f):
        step = span // EACH
        return jnp.concatenate(
            [
                x[c * step : (c + 1) * step, (f * EACH + c) * LANES : (f * EACH + c + 1) * LANES]
                for c in range(EACH)
            ],
            0,
        )

    def post(r, f, edge):
        edge = edge.astype(BF16)
        for g in range(n * BLOCK // 256):
            block = dot(psend[g * 256 : (g + 1) * 256, :], edge)
            send[r, f, g * (256 // BLOCK) : (g + 1) * (256 // BLOCK)] = block.reshape(
                256 // BLOCK, BLOCK, LANES
            ).astype(BF16)

        for p in partners:
            pltpu.make_async_remote_copy(
                src_ref=send.at[r, f, p[0] * n_shard + p[1]],
                dst_ref=recv.at[r, f, me],
                send_sem=send_sem.at[r, f],
                recv_sem=recv_sem.at[r, f],
                device_id=p,
                device_id_type=MESH,
            ).start()
        pltpu.make_async_copy(send.at[r, f, me], recv.at[r, f, me], recv_sem.at[r, f]).start()

    first = dot(edge_of(iota((n_edge, rows), 1)), feat[...])
    pl.semaphore_wait(barrier, n - 1)
    for f in range(HALVES):
        post(0, f, diagonal(first, f))

    to_scalars.wait()
    loads[0].wait()
    total[0] = jnp.zeros((size, size), F32)

    def gather_slot(t, carry):
        total[t + 1] = total[jnp.clip(link_at[0, t], 0, slots)] + tiles[0, t].astype(F32)
        return carry

    lax.fori_loop(0, slots, gather_slot, 0)
    for r in range(row_tiles):
        for c in range(col_tiles):
            adj[r * size : (r + 1) * size, c * size : (c + 1) * size] = total[
                jnp.clip(link_at[1, r * col_tiles + c], 0, slots)
            ].astype(BF16)

    place_t = onehot(iota((rows, rows), 0) == order[...])
    place = place_t.astype(F32).T.astype(BF16)
    hops[0] = dot(place, feat[...]).astype(BF16)
    adj_own[...] = dot(dot(place, adj[:, :rows]).astype(BF16), place_t).astype(BF16)
    adj_halo[...] = dot(place, adj[:, rows:]).astype(BF16)
    edge = edge_of(order[...])
    own_edge[...] = dot(edge, adj_own[...]).astype(BF16)
    halo_part = dot(edge, adj_halo[...]).astype(BF16)
    group = LANES // n_pick
    shape = (LANES, LANES * EACH)
    widen = onehot(
        (iota(shape, 0) // n_pick == iota(shape, 1) // BLOCK)
        & (lax.rem(iota(shape, 0), n_pick) == lax.rem(iota(shape, 1), n_pick))
    )
    shape = (span, LANES * EACH)
    same = iota(shape, 0) // (span // EACH) == lax.rem(iota(shape, 1) // n_pick, EACH)
    for g in range(n // group):
        wide = dot(halo_part[:, g * LANES : (g + 1) * LANES], widen)
        halo_edge[:, g * LANES * EACH : (g + 1) * LANES * EACH] = jnp.where(same, wide, 0.0).astype(BF16)

    def source(i):
        head = lax.rem(i // (LANES // HEADS), HEADS)
        return head * (width // HEADS) + (i // LANES) * (LANES // HEADS) + lax.rem(i, LANES // HEADS)

    shape = (width, width)
    by_row = onehot(iota(shape, 1) == source(iota(shape, 0)))
    by_col = onehot(iota(shape, 0) == source(iota(shape, 1)))
    loads[1].wait()
    for i in range(3):
        attn[0, i] = dot(attn[0, i], by_col).astype(BF16)
    attn[0, 3] = dot(by_row, attn[0, 3]).astype(BF16)

    per = 256 // BLOCK
    shape = (256, 256)
    row, col = iota(shape, 0), iota(shape, 1)
    regroup = onehot(
        (lax.rem(row // n_pick, per) == col // BLOCK)
        & (row // (256 // EACH) == lax.rem(col // n_pick, EACH))
        & (lax.rem(row, n_pick) == lax.rem(col, n_pick))
    )

    shape = (2 * LANES, 2 * LANES)
    seg = LANES // HEADS
    gather = jnp.where(
        iota(shape, 0) // seg == iota(shape, 1) // seg, (width // HEADS) ** -0.5, 0.0
    ).astype(BF16)

    def lanes(c):
        return slice(c * LANES, (c + 1) * LANES)

    def project(h):
        for b in range(rows // 256):
            at = slice(b * 256, (b + 1) * 256)
            a = layer_norm(hops[h, at, :].astype(F32), gain[0, 0:1, :]).astype(BF16)
            q[h, at, :] = dot(a, attn[0, 0]).astype(BF16)
            k[h, at, :] = dot(a, attn[0, 1]).astype(BF16)
            v[h, at, :] = dot(a, attn[0, 2])

        def against(j, carry):
            for b in range(rows // CHUNK):
                at = slice(b * CHUNK, (b + 1) * CHUNK)

                def product(x, y):
                    p = [q[x, at, lanes(c)] * k[y, at, lanes(c)] for c in range(PARTS)]
                    return (p[0] + p[1]) + (p[2] + p[3])

                score[h, j, at, :] = dot(jnp.concatenate([product(h, j), product(j, h)], 1), gather)
            return carry

        lax.fori_loop(0, h + 1, against, 0)

    def arrived(r, f):
        pltpu.make_async_copy(recv.at[r, f], recv.at[r, f], recv_sem.at[r, f]).wait()
        return recv[r, f].astype(F32).reshape(n * BLOCK, LANES).astype(BF16)

    def advance(r, f, got):
        part = 256 // EACH
        for g in range(n * BLOCK // 512):
            both = jnp.concatenate([got[g * 512 : g * 512 + 256], got[g * 512 + 256 : (g + 1) * 512]], 1)
            moved = dot(regroup, both).astype(BF16)
            for c in range(EACH):
                for d in range(2):
                    halo[f, (2 * g + d) * part : (2 * g + d + 1) * part, lanes(c)] = moved[
                        c * part : (c + 1) * part, lanes(d)
                    ]
        at = slice(f * EACH * LANES, (f + 1) * EACH * LANES)
        hops[r + 1, :, at] = (own[:, at] + dot(adj_halo[...], halo[f])).astype(BF16)

    def prepare(r):
        own[...] = dot(adj_own[...], hops[r])
        project(r)

    def hop(r, carry):
        own_part = dot(own_edge[...], hops[r])
        for f in range(HALVES):
            own_diag[f] = diagonal(own_part, f)
        prepare(r)
        for f in range(HALVES):
            got = arrived(r, f)
            post(r + 1, f, own_diag[f] + dot(halo_edge[...], got))
            advance(r, f, got)
        return carry

    lax.fori_loop(0, HOPS - 1, hop, 0)
    prepare(HOPS - 1)
    for f in range(HALVES):
        advance(HOPS - 1, f, arrived(HOPS - 1, f))
    project(HOPS)
    loads[2].wait()
    loads[3].wait()

    share = rows // n_shard
    n_chunk = rows // CHUNK
    side = CHUNK // share

    def chunk_at(step):
        return lax.rem(shard // side + (2, 3, 1, 0)[step], n_chunk)

    def mix(step, blocks):
        base = chunk_at(step) * CHUNK
        for b in blocks:
            at = pl.ds(pl.multiple_of(base + b * SUB, SUB), SUB)
            for i in range(TOKENS):
                s = [
                    score[max(i, j), min(i, j), at, lanes(0 if i >= j else 1)]
                    for j in range(TOKENS)
                ]
                top = functools.reduce(jnp.maximum, s)
                e = [jnp.exp(x - top) for x in s]
                scale = 1.0 / functools.reduce(jnp.add, e)
                w = [x * scale for x in e]
                to = slice(i * CHUNK + b * SUB, i * CHUNK + (b + 1) * SUB)
                for c in range(PARTS):
                    acc = w[0] * v[0, at, lanes(c)]
                    for j in range(1, TOKENS):
                        acc += w[j] * v[j, at, lanes(c)]
                    ctx[step % 2, to, lanes(c)] = acc.astype(BF16)

    def finish(step):
        at_chunk = chunk_at(step)
        at = pl.ds(pl.multiple_of(at_chunk * CHUNK, CHUNK), CHUNK)
        two = step % 2
        z0 = hid[two, 0:CHUNK, :]
        base_score = jnp.sum(z0 * readw[0:1, :], -1, keepdims=True)
        s = [
            base_score + jnp.sum(hid[two, i * CHUNK : (i + 1) * CHUNK, :] * readw[1:2, :], -1, keepdims=True)
            for i in range(1, TOKENS)
        ]
        top = functools.reduce(jnp.maximum, s)
        e = [jnp.exp(x - top) for x in s]
        scale = 1.0 / functools.reduce(jnp.add, e)
        state = z0
        for i in range(1, TOKENS):
            state += (e[i - 1] * scale) * hid[two, i * CHUNK : (i + 1) * CHUNK, :]
        stage[at, :] = state.astype(BF16)

        dst = out.at[pl.ds(pl.multiple_of(shard * share, share), share)]
        for far in (2, 3, 1, 0):
            to = at_chunk * side + lax.rem(lax.rem(shard, side) + far, side)
            src = stage.at[pl.ds(pl.multiple_of(to * share, share), share)]
            if step == n_chunk - 1 and far == 0:
                pltpu.make_async_copy(src, dst, out_recv_sem).start()
            else:
                pltpu.make_async_remote_copy(
                    src_ref=src,
                    dst_ref=dst,
                    send_sem=out_send_sem,
                    recv_sem=out_recv_sem,
                    device_id=(dom, to),
                    device_id_type=MESH,
                ).start()

    def layer(step):
        at_chunk = chunk_at(step)
        base = at_chunk * CHUNK
        at = pl.ds(pl.multiple_of(base, CHUNK), CHUNK)
        two = step % 2
        hid[two] = dot(ctx[two], attn[0, 3])
        if step > 0:
            finish(step - 1)
        for i in range(TOKENS):
            to = slice(i * CHUNK, (i + 1) * CHUNK)
            h = hops[i, at, :].astype(F32) + hid[two, to, :]
            hid[two, to, :] = h
            norm[two, to, :] = layer_norm(h, gain[0, 1:2, :]).astype(BF16)
        blocks = mid.shape[2] // 256
        subs = CHUNK // SUB
        for b in range(blocks):
            x = dot(norm[two], fin[0, :, b * 256 : (b + 1) * 256])
            if step + 1 < n_chunk:
                mix(step + 1, range(b * subs // blocks, (b + 1) * subs // blocks))
            mid[two, :, b * 256 : (b + 1) * 256] = jax.nn.gelu(x, approximate=True).astype(BF16)
        hid[two] += dot(mid[two], fout[0])

    mix(0, range(CHUNK // SUB))
    for step in range(n_chunk):
        layer(step)
    finish(n_chunk - 1)

    sent = send.at[0, 0, pl.ds(0, n - 1)]
    for r in range(HOPS):
        for f in range(HALVES):
            pltpu.make_async_copy(sent, sent, send_sem.at[r, f]).wait()
    sent = stage.at[pl.ds(0, rows - share)]
    pltpu.make_async_copy(sent, sent, out_send_sem).wait()
    pltpu.make_async_copy(out, out, out_recv_sem).wait()


def local(
    features,
    tile_values,
    tile_coords,
    tile_count,
    boundary_index,
    peer_pick,
    shuffle_order,
    attn_weight,
    ffn_in,
    ffn_out,
    norm_gain,
    read_weight,
):
    rows, width = features.shape
    size = tile_values.shape[2]
    n, n_pick = peer_pick.shape[1], peer_pick.shape[2]
    halo_rows = n * n_pick
    hidden = ffn_in.shape[2]
    vmem = pl.BlockSpec(memory_space=pltpu.VMEM)
    smem = pl.BlockSpec(memory_space=pltpu.SMEM)
    hbm = pl.BlockSpec(memory_space=pl.ANY)
    message = n * BLOCK
    span = BLOCK * boundary_index.shape[1]
    states = pl.pallas_call(
        window,
        out_shape=jax.ShapeDtypeStruct((rows, width), BF16),
        in_specs=[vmem, vmem, smem, smem, vmem, vmem, hbm, hbm, hbm, hbm, vmem, vmem],
        out_specs=hbm,
        scratch_shapes=[
            pltpu.VMEM((TOKENS, rows, width), BF16),
            pltpu.VMEM((HOPS, HALVES, n, BLOCK, LANES), BF16),
            pltpu.VMEM((HOPS, HALVES, n, BLOCK, LANES), BF16),
            pltpu.VMEM((message, span), BF16),
            pltpu.VMEM((span, rows), BF16),
            pltpu.VMEM((span, message), BF16),
            pltpu.VMEM((rows, rows), BF16),
            pltpu.VMEM((rows, halo_rows), BF16),
            pltpu.VMEM((HALVES, halo_rows, EACH * LANES), BF16),
            pltpu.VMEM((rows, width), F32),
            pltpu.VMEM((HALVES, span, LANES), F32),
            pltpu.VMEM((TOKENS, rows, width), BF16),
            pltpu.VMEM((TOKENS, rows, width), BF16),
            pltpu.VMEM((TOKENS, rows, width), F32),
            pltpu.VMEM(attn_weight.shape, BF16),
            pltpu.VMEM(ffn_in.shape, BF16),
            pltpu.VMEM(ffn_out.shape, BF16),
            pltpu.VMEM(tile_values.shape, BF16),
            pltpu.VMEM((tile_values.shape[1] + 1, size, size), F32),
            pltpu.VMEM((8, LANES), I32),
            pltpu.SMEM((8, LANES), I32),
            pltpu.VMEM((rows, rows + halo_rows), BF16),
            pltpu.VMEM((TOKENS, TOKENS, rows, 2 * LANES), F32),
            pltpu.VMEM((2, TOKENS * CHUNK, width), BF16),
            pltpu.VMEM((2, TOKENS * CHUNK, width), BF16),
            pltpu.VMEM((2, TOKENS * CHUNK, width), F32),
            pltpu.VMEM((2, TOKENS * CHUNK, hidden), BF16),
            pltpu.VMEM((rows, width), BF16),
            pltpu.SemaphoreType.DMA((HOPS, HALVES)),
            pltpu.SemaphoreType.DMA((HOPS, HALVES)),
            pltpu.SemaphoreType.DMA((4,)),
            pltpu.SemaphoreType.DMA,
            pltpu.SemaphoreType.DMA,
            pltpu.SemaphoreType.DMA,
        ],
        compiler_params=pltpu.CompilerParams(
            collective_id=0, has_side_effects=True, vmem_limit_bytes=56 * 2**20
        ),
        name="window",
    )(
        features,
        jnp.swapaxes(tile_coords, 1, 2),
        tile_count.reshape(1, 1),
        boundary_index,
        jnp.swapaxes(peer_pick, 1, 2),
        shuffle_order,
        tile_values,
        attn_weight,
        ffn_in,
        ffn_out,
        norm_gain,
        read_weight,
    )
    return states


def solution(mesh):
    placed = (
        P(("dom", "shard"), None),
        P(("dom", "shard"), None, None, None),
        P(("dom", "shard"), None, None),
        P(("dom", "shard")),
        P(("dom", "shard"), None),
        P(("dom", "shard"), None, None),
        P(("dom", "shard"), None),
        P(),
        P(),
        P(),
        P(),
        P(),
    )
    return jax.shard_map(
        local, mesh=mesh, in_specs=placed, out_specs=P(("dom", "shard"), None), check_vma=False
    )
```
